32 devices in a mesh: groups: 2 (over y), mz: 4 (over z), pix: 4 (over x, core).
Axes of the slice: x: 2, y: 2, z: 4, core: 2. Of those that a mesh axis runs over, the one named last changes fastest.
Arguments:
- spectra: bfloat16 [1024, 262144], P(('groups', 'pix'), 'mz'), parts along dimension 0
- kernel: bfloat16 [129], replicated, may hold values from 0.0009994507 to 0.029907227
- probes: bfloat16 [262144, 128], P('mz'), may hold values from -0.01171875 to 0.01171875
Outputs:
- basis: bfloat16 [1024, 128], P(('groups', 'pix')), parts along dimension 0
- projected: bfloat16 [256, 262144], P(('groups', 'pix'), 'mz'), parts along dimension 0
The draws below stay inside these ranges and needn't reach their ends.
There are 2 independent parts, one for each index of `groups`. The reference program is written for one: setup_inputs(seed, part) draws one part's arguments, and reference() takes and returns one part's arrays. A program takes and returns all parts, laid end to end along the dimension named above; an argument that names none is the same for every part. Nothing has to cross between parts.
All inputs are finite; a program needn't handle non-finite values.
Results may differ from the reference program's by a relative error of at most 0.019.
Values may be sent and summed in bfloat16 or wider, within the bound.
A program may use at most 192 MiB of HBM per device.

```python
import math
import jax
import jax.numpy as jnp
from jax import lax

BINS = 262144
PROBES = 128
BAND = 129
PIX_DEV = 128
PIXELS = 512
N_PIX = 4


def draw_spectra(key, part):
    first, second = jax.random.split(key, 2)
    phase = jax.random.uniform(second, (PIXELS, 1), jnp.float32) * 6.283
    position = jnp.arange(BINS, dtype=jnp.float32)[None, :]
    smooth = 1.5 + jnp.sin(position * (6.283 / 4096.0) + phase)
    rough = jax.random.normal(first, (PIXELS, BINS), jnp.float32)
    values = rough + smooth
    return values.astype(jnp.bfloat16)


def steps_of(rng, dims, cuts, low, high):
    def one(dim, shards_of):
        heights = jax.random.uniform(jax.random.fold_in(jax.random.fold_in(rng, 6), dim), (shards_of,), jnp.float32, low / len(cuts), high / len(cuts))
        return jnp.repeat(jnp.exp(heights), dims[dim] // shards_of).reshape((-1,) + (1,) * (len(dims) - dim - 1))

    factor_of = one(*cuts[0])
    for cut in cuts[1:]:
        factor_of = factor_of * one(*cut)
    return factor_of


def noise(stream_key, dims, width, bound, pieces=(), kind=jnp.bfloat16):
    values = width * jax.random.normal(stream_key, dims, jnp.float32)
    if pieces:
        values = values * steps_of(stream_key, dims, pieces, -0.22, 0.18)
    return jnp.clip(values, -bound, bound).astype(kind)


def setup_inputs(seed: int = 0, part: int = 0) -> dict:
    key_of = jax.random.split(jax.random.key(seed), 4)
    own_keys = jax.random.split(jax.random.fold_in(key_of[3], part), 4)
    spectra = draw_spectra(jax.random.fold_in(jax.random.fold_in(key_of[3], part), 71), part)
    kernel = jnp.clip(jnp.exp(jax.random.uniform(key_of[1], (BAND,), jnp.float32, math.log(0.0009994507), math.log(0.029907227))), 0.0009994507, 0.029907227).astype(jnp.bfloat16)
    probes = noise(key_of[2], (BINS, PROBES), BINS ** -0.5, 0.01171875, ((0, 4),))
    return {"spectra": spectra, "kernel": kernel, "probes": probes}


def smooth_block(rows, kernel):
    lhs = rows.astype(jnp.float32)[:, None, :]
    rhs = kernel.astype(jnp.float32)[None, None, :]
    base = lax.conv_general_dilated(lhs, rhs, (1,), ((64, 64),), dimension_numbers=('NCH', 'OIH', 'NCH'), precision=lax.Precision.HIGHEST)[:, 0, :]
    return (rows.astype(jnp.float32) - base).astype(jnp.bfloat16)

def reference(spectra, kernel, probes):
    blocks = spectra.reshape(N_PIX, PIX_DEV, BINS)
    cleaned_blocks = lax.map(lambda rows: smooth_block(rows, kernel), blocks)
    cleaned = cleaned_blocks.reshape(PIXELS, BINS)
    sketch = jnp.dot(cleaned.astype(jnp.float32), probes.astype(jnp.float32), preferred_element_type=jnp.float32)
    gram = jnp.dot(sketch.T, sketch, precision=lax.Precision.HIGHEST) / float(PIXELS)
    lower = jnp.linalg.cholesky(gram)
    basis_f = lax.linalg.triangular_solve(lower, sketch, left_side=False, lower=True, transpose_a=True)
    basis = basis_f.astype(jnp.bfloat16)
    factor = 1.0 / math.sqrt(float(PIXELS))
    total = jnp.zeros((PROBES, BINS), jnp.float32)
    for index in range(N_PIX):
        rows = basis[index * PIX_DEV:(index + 1) * PIX_DEV]
        part_sum = jnp.dot(rows.T.astype(jnp.float32), cleaned_blocks[index].astype(jnp.float32), preferred_element_type=jnp.float32) * factor
        total = total + part_sum.astype(jnp.bfloat16).astype(jnp.float32)
    return (basis, total.astype(jnp.bfloat16))
```

```python
import functools
import math

import jax
import jax.numpy as jnp
from jax import lax
from jax.experimental import pallas as pl
from jax.experimental.pallas import tpu as pltpu
from jax.sharding import PartitionSpec as P

LANES = 128
OUT = 256
WIN = OUT + 2 * LANES


def clean_kernel(steps, main, left, right, halo_l, halo_r, u_ref, probes, cleaned, sketch, w_ref):
    step = pl.program_id(0)
    tile = main.shape[1]

    @pl.when(step == 0)
    def _():
        base = jnp.broadcast_to(u_ref[...], (WIN, WIN))
        w_ref[...] = pltpu.roll(base, 0, 1, stride=1, stride_axis=0)[:, :OUT].astype(jnp.bfloat16)
        sketch[...] = jnp.zeros_like(sketch)

    low = jnp.where(step == 0, halo_l[...], left[...])
    high = jnp.where(step == steps - 1, halo_r[...], right[...])
    w = w_ref[...]
    count = tile // OUT
    for j in range(count):
        pieces = []
        begin, end = j * OUT - LANES, (j + 1) * OUT + LANES
        if begin < 0:
            pieces.append(low)
        pieces.append(main[:, max(begin, 0) : min(end, tile)])
        if end > tile:
            pieces.append(high)
        window = pieces[0] if len(pieces) == 1 else jnp.concatenate(pieces, axis=1)
        base = jnp.dot(window, w, preferred_element_type=jnp.float32)
        mine = main[:, j * OUT : (j + 1) * OUT].astype(jnp.float32)
        cleaned[:, j * OUT : (j + 1) * OUT] = (mine - base).astype(jnp.bfloat16)
    sketch[...] += jnp.dot(cleaned[...], probes[...], preferred_element_type=jnp.float32)


def clean_and_sketch(spectra, halo_l, halo_r, u, probes):
    rows, bins = spectra.shape
    cols = probes.shape[1]
    tile = min(4096, bins)
    steps = bins // tile
    per = tile // LANES
    last = bins // LANES - 1
    return pl.pallas_call(
        functools.partial(clean_kernel, steps),
        grid=(steps,),
        in_specs=[
            pl.BlockSpec((rows, tile), lambda i: (0, i)),
            pl.BlockSpec((rows, LANES), lambda i: (0, jnp.maximum(i * per - 1, 0))),
            pl.BlockSpec((rows, LANES), lambda i: (0, jnp.minimum((i + 1) * per, last))),
            pl.BlockSpec((rows, LANES), lambda i: (0, 0)),
            pl.BlockSpec((rows, LANES), lambda i: (0, 0)),
            pl.BlockSpec((1, WIN), lambda i: (0, 0)),
            pl.BlockSpec((tile, cols), lambda i: (i, 0)),
        ],
        out_specs=[
            pl.BlockSpec((rows, tile), lambda i: (0, i)),
            pl.BlockSpec((rows, cols), lambda i: (0, 0)),
        ],
        out_shape=[
            jax.ShapeDtypeStruct((rows, bins), jnp.bfloat16),
            jax.ShapeDtypeStruct((rows, cols), jnp.float32),
        ],
        scratch_shapes=[pltpu.VMEM((WIN, OUT), jnp.bfloat16)],
        compiler_params=pltpu.CompilerParams(
            dimension_semantics=("arbitrary",), vmem_limit_bytes=32 * 2**20
        ),
        cost_estimate=pl.CostEstimate(
            flops=2 * rows * bins * (WIN + cols),
            bytes_accessed=bins * (4 * rows + 2 * cols),
            transcendentals=0,
        ),
    )(spectra, spectra, spectra, halo_l, halo_r, u, probes)


def project_kernel(
    n_pix, factor, basis_t, cleaned, out,
    rows_in, lhs, give, core_in, hold, x_give, x_in, acc, out_v,
    load_sem, give_sem, core_sem, x_send_sem, x_recv_sem, store_sem,
):
    chips = n_pix // 2
    share = basis_t.shape[1]
    half = chips * share
    chunks, width = acc.shape[0], acc.shape[2]
    ring = give.shape[0]
    groups, mz, pix = lax.axis_index("groups"), lax.axis_index("mz"), lax.axis_index("pix")
    core = lax.rem(pix, 2)
    chip = lax.div(pix, 2)
    other = 1 - core

    def device(at_chip, at_core):
        return (groups, mz, at_chip * 2 + at_core)

    def chip_of(d):
        return lax.rem(chip + d, chips)

    def load(k):
        return pltpu.make_async_copy(
            cleaned.at[:, pl.ds(pl.multiple_of(k * width, width), width)],
            rows_in.at[k], load_sem.at[k],
        )

    @pl.loop(0, chunks)
    def _(k):
        load(k).start()

    barrier = pltpu.get_barrier_semaphore()
    pl.semaphore_signal(barrier, inc=1, device_id=device(chip, other), device_id_type=pl.DeviceIdType.MESH)
    for d in range(1, chips):
        pl.semaphore_signal(
            barrier, inc=1, device_id=device(chip_of(d), core), device_id_type=pl.DeviceIdType.MESH
        )

    for d in range(chips):
        lhs[pl.ds(d * share, share), :] = basis_t[chip_of(d) * 2 + other]
        lhs[pl.ds(half + d * share, share), :] = basis_t[chip_of(d) * 2 + core]

    pl.semaphore_wait(barrier, chips)

    def to_core(k):
        return pltpu.make_async_remote_copy(
            src_ref=give.at[lax.rem(k, ring)], dst_ref=core_in.at[k],
            send_sem=give_sem.at[lax.rem(k, ring)], recv_sem=core_sem.at[k],
            device_id=device(chip, other), device_id_type=pl.DeviceIdType.MESH,
        )

    def to_chip(d, k):
        return pltpu.make_async_remote_copy(
            src_ref=x_give.at[d - 1, k], dst_ref=x_in.at[d - 1, k],
            send_sem=x_send_sem.at[d - 1, k], recv_sem=x_recv_sem.at[d - 1, k],
            device_id=device(chip_of(d), core), device_id_type=pl.DeviceIdType.MESH,
        )

    def first(k):
        load(k).wait()
        slot = lax.rem(k, ring)

        @pl.when(k >= ring)
        def _():
            to_core(k - ring).wait_send()

        part = jnp.dot(lhs[...], rows_in[k], preferred_element_type=jnp.float32) * factor
        part = part.astype(jnp.bfloat16)
        give[slot] = part[:half]
        to_core(k).start()
        hold[slot] = part[half:]

    def second(k):
        to_core(k).wait_recv()
        slot = lax.rem(k, ring)
        total = hold[slot].astype(jnp.float32) + core_in[k].astype(jnp.float32)
        acc[k] = total[:share]
        for d in range(1, chips):
            x_give[d - 1, k] = total[d * share : (d + 1) * share].astype(jnp.bfloat16)
            to_chip(d, k).start()

    def store(k):
        return pltpu.make_async_copy(
            out_v.at[k], out.at[:, pl.ds(pl.multiple_of(k * width, width), width)], store_sem.at[k]
        )

    lag = min(ring - 1, chunks)

    @pl.loop(0, lag)
    def _(k):
        first(k)

    @pl.loop(lag, chunks)
    def _(k):
        first(k)
        second(k - lag)

    @pl.loop(chunks - lag, chunks)
    def _(k):
        second(k)

    @pl.loop(max(chunks - ring, 0), chunks)
    def _(k):
        to_core(k).wait_send()

    @pl.loop(0, chunks)
    def _(k):
        total = acc[k]
        for d in range(1, chips):
            to_chip(d, k).wait()
            total = total + x_in[d - 1, k].astype(jnp.float32)
        out_v[k] = total.astype(jnp.bfloat16)
        store(k).start()

    @pl.loop(0, chunks)
    def _(k):
        store(k).wait()


def project(basis, cleaned, n_pix, factor):
    rows, bins = cleaned.shape
    cols = basis.shape[1]
    share = cols // n_pix
    chips = n_pix // 2
    half = chips * share
    width = min(2048, bins)
    chunks = bins // width
    ring = 4
    bf16, f32 = jnp.bfloat16, jnp.float32
    basis_t = basis.T.reshape(n_pix, share, rows)
    away = max(chips - 1, 1)
    return pl.pallas_call(
        functools.partial(project_kernel, n_pix, factor),
        in_specs=[pl.BlockSpec(memory_space=pltpu.VMEM), pl.BlockSpec(memory_space=pl.ANY)],
        out_specs=pl.BlockSpec(memory_space=pl.ANY),
        out_shape=jax.ShapeDtypeStruct((share, bins), bf16),
        scratch_shapes=[
            pltpu.VMEM((chunks, rows, width), bf16),
            pltpu.VMEM((cols, rows), bf16),
            pltpu.VMEM((ring, half, width), bf16),
            pltpu.VMEM((chunks, half, width), bf16),
            pltpu.VMEM((ring, half, width), bf16),
            pltpu.VMEM((away, chunks, share, width), bf16),
            pltpu.VMEM((away, chunks, share, width), bf16),
            pltpu.VMEM((chunks, share, width), f32),
            pltpu.VMEM((chunks, share, width), bf16),
            pltpu.SemaphoreType.DMA((chunks,)),
            pltpu.SemaphoreType.DMA((ring,)),
            pltpu.SemaphoreType.DMA((chunks,)),
            pltpu.SemaphoreType.DMA((away, chunks)),
            pltpu.SemaphoreType.DMA((away, chunks)),
            pltpu.SemaphoreType.DMA((chunks,)),
        ],
        compiler_params=pltpu.CompilerParams(
            collective_id=0, has_side_effects=True, vmem_limit_bytes=56 * 2**20
        ),
        cost_estimate=pl.CostEstimate(
            flops=2 * rows * bins * cols,
            bytes_accessed=2 * bins * (rows + share),
            transcendentals=0,
        ),
    )(basis_t, cleaned)


def per_device(spectra, kernel, probes):
    pix_rows, bin_cols = spectra.shape
    n_pix, n_mz = lax.axis_size("pix"), lax.axis_size("mz")
    all_pixels = pix_rows * n_pix
    factor = 1.0 / math.sqrt(float(all_pixels))
    up = [(i, i + 1) for i in range(n_mz - 1)]
    down = [(b, a) for a, b in up]
    halo_l = lax.ppermute(spectra[:, bin_cols - LANES :], "mz", up)
    halo_r = lax.ppermute(spectra[:, :LANES], "mz", down)
    taps = kernel.shape[0]
    low = WIN - (LANES - taps // 2) - (taps - 1)
    u = jnp.pad(kernel[::-1].astype(jnp.float32), (low, WIN - low - taps))[None, :]
    cleaned, partial_sketch = clean_and_sketch(spectra, halo_l, halo_r, u, probes)
    inner_dims = (((0,), (0,)), ((), ()))
    sketch = lax.psum(partial_sketch, "mz")
    local_gram = lax.dot_general(sketch, sketch, inner_dims, precision=lax.Precision.HIGHEST)
    gram = lax.psum(local_gram, "pix") / float(all_pixels)
    lower = jnp.linalg.cholesky(gram)
    basis = lax.linalg.triangular_solve(
        lower, sketch, left_side=False, lower=True, transpose_a=True
    ).astype(jnp.bfloat16)
    projected = project(basis, cleaned, n_pix, factor)
    return (basis, projected)


def solution(mesh):
    in_specs = (P(("groups", "pix"), "mz"), P(), P("mz", None))
    out_specs = (P(("groups", "pix"), None), P(("groups", "pix"), "mz"))
    return jax.shard_map(
        per_device, mesh=mesh, in_specs=in_specs, out_specs=out_specs, check_vma=False
    )
```

```python
import functools
import math

import jax
import jax.numpy as jnp
from jax import lax
from jax.experimental import pallas as pl
from jax.experimental.pallas import tpu as pltpu
from jax.sharding import PartitionSpec as P

LANES = 128
OUT = 256
WIN = OUT + 2 * LANES


MESH = pl.DeviceIdType.MESH
HIGHEST = lax.Precision.HIGHEST
PANEL = 8


def whiten(a_ref, x_ref):
    size = a_ref.shape[0]
    row = lax.broadcasted_iota(jnp.int32, (PANEL, 1), 0)
    x_ref[...] = (
        lax.broadcasted_iota(jnp.int32, (size, size), 0)
        == lax.broadcasted_iota(jnp.int32, (size, size), 1)
    ).astype(jnp.float32)

    def panel(index, carry):
        a, x = carry
        p, q = a[:PANEL], x[:PANEL]
        rows_p, rows_q = [], []
        for t in range(PANEL):
            inv = lax.rsqrt(p[t : t + 1, t : t + 1])
            r, y = p[t : t + 1] * inv, q[t : t + 1] * inv
            rows_p.append(r)
            rows_q.append(y)
            if t + 1 < PANEL:
                scale = jnp.where(row > t, p[:, t : t + 1] * inv, 0.0)
                p = p - scale * r
                q = q - scale * y
        r, y = jnp.concatenate(rows_p, axis=0), jnp.concatenate(rows_q, axis=0)
        x_ref[pl.ds(pl.multiple_of(index * PANEL, PANEL), PANEL), :] = y
        turned = r.T
        rest_a, rest_x = a[PANEL:], x[PANEL:]
        for t in range(PANEL):
            scale = turned[PANEL:, t : t + 1]
            rest_a = rest_a - scale * r[t : t + 1]
            rest_x = rest_x - scale * y[t : t + 1]
        zeros = jnp.zeros((PANEL, size), jnp.float32)
        rest_a = pltpu.roll(rest_a, size - PANEL, 1)
        return jnp.concatenate([rest_a, zeros], axis=0), jnp.concatenate([rest_x, zeros], axis=0)

    lax.fori_loop(0, size // PANEL, panel, (a_ref[...], x_ref[...]))


def fused_kernel(
    n_mz, n_pix, factor, pixels, spectra, u_ref, probes, basis, out,
    raw, tap, w_ref, halo, cleaned, total, parts, parts_in, sketch, gram, gram_in, x_ref,
    lhs, give, core_in, hold, x_give, x_in, acc, out_v,
    raw_sem, tap_sem, halo_send, halo_recv, parts_send, parts_recv, all_send, all_recv,
    gram_send, gram_recv, give_sem, core_sem, x_send_sem, x_recv_sem, store_sem,
):
    bins = spectra.shape[1]
    slots, tile = tap.shape[0], tap.shape[1]
    tiles = bins // tile
    chips = n_pix // 2
    share = lhs.shape[0] // n_pix
    half = chips * share
    chunks, width = acc.shape[0], acc.shape[2]
    per = tile // width
    ring = give.shape[0]
    groups, mz, pix = lax.axis_index("groups"), lax.axis_index("mz"), lax.axis_index("pix")
    core = lax.rem(pix, 2)
    chip = lax.div(pix, 2)
    other = 1 - core

    def at_z(d):
        return (groups, lax.rem(mz + d, n_mz), pix)

    def at_pix(d):
        return (groups, mz, lax.rem(pix + d, n_pix))

    def device(at_chip, at_core):
        return (groups, mz, at_chip * 2 + at_core)

    def chip_of(d):
        return lax.rem(chip + d, chips)

    def tile_of(pos):
        return jnp.where(pos == tiles - 1, tiles - 1, jnp.where(pos == tiles - 2, 0, pos + 1))

    def each_load(pos, act):
        slot = lax.rem(pos, slots)

        @pl.when(pos < tiles - 2)
        def _():
            begin = pl.multiple_of((pos + 1) * tile - LANES, LANES)
            act(pltpu.make_async_copy(
                spectra.at[:, pl.ds(begin, tile + 2 * LANES)], raw.at[slot], raw_sem.at[slot]))

        @pl.when(pos == tiles - 2)
        def _():
            act(pltpu.make_async_copy(
                spectra.at[:, pl.ds(0, tile + LANES)],
                raw.at[slot, :, pl.ds(LANES, tile + LANES)], raw_sem.at[slot]))

        @pl.when(pos == tiles - 1)
        def _():
            act(pltpu.make_async_copy(
                spectra.at[:, pl.ds(bins - tile - LANES, tile + LANES)],
                raw.at[slot, :, pl.ds(0, tile + LANES)], raw_sem.at[slot]))

        begin = pl.multiple_of(tile_of(pos) * tile, tile)
        act(pltpu.make_async_copy(probes.at[pl.ds(begin, tile), :], tap.at[slot], tap_sem.at[slot]))

    for pos in range(min(slots, tiles)):
        each_load(jnp.int32(pos), lambda c: c.start())

    barrier = pltpu.get_barrier_semaphore()
    for d in range(1, n_mz):
        pl.semaphore_signal(barrier, inc=1, device_id=at_z(d), device_id_type=MESH)
    for d in range(1, n_pix):
        pl.semaphore_signal(barrier, inc=1, device_id=at_pix(d), device_id_type=MESH)

    base = jnp.broadcast_to(u_ref[...], (WIN, WIN))
    w_ref[...] = pltpu.roll(base, 0, 1, stride=1, stride_axis=0)[:, :OUT].astype(jnp.bfloat16)
    total[...] = jnp.zeros_like(total)

    pl.semaphore_wait(barrier, n_mz - 1 + n_pix - 1)

    to_right = pltpu.make_async_remote_copy(
        src_ref=spectra.at[:, pl.ds(bins - LANES, LANES)], dst_ref=halo.at[0],
        send_sem=halo_send.at[0], recv_sem=halo_recv.at[0],
        device_id=at_z(1), device_id_type=MESH,
    )
    to_left = pltpu.make_async_remote_copy(
        src_ref=spectra.at[:, pl.ds(0, LANES)], dst_ref=halo.at[1],
        send_sem=halo_send.at[1], recv_sem=halo_recv.at[1],
        device_id=at_z(n_mz - 1), device_id_type=MESH,
    )

    @pl.when(mz < n_mz - 1)
    def _():
        to_right.start()

    @pl.when(mz > 0)
    def _():
        to_left.start()

    @pl.when(mz == 0)
    def _():
        halo[0] = jnp.zeros(halo.shape[1:], halo.dtype)

    @pl.when(mz == n_mz - 1)
    def _():
        halo[1] = jnp.zeros(halo.shape[1:], halo.dtype)

    def clean(pos):
        slot = lax.rem(pos, slots)
        at = tile_of(pos)
        each_load(pos, lambda c: c.wait())

        @pl.when(pos == tiles - 2)
        def _():
            @pl.when(mz > 0)
            def _():
                to_right.wait_recv()

            raw[slot, :, :LANES] = halo[0]

        @pl.when(pos == tiles - 1)
        def _():
            @pl.when(mz < n_mz - 1)
            def _():
                to_left.wait_recv()

            raw[slot, :, tile + LANES :] = halo[1]

        w = w_ref[...]
        done = []
        for j in range(tile // OUT):
            window = raw[slot, :, j * OUT : j * OUT + WIN]
            smooth = jnp.dot(window, w, preferred_element_type=jnp.float32)
            mine = raw[slot, :, LANES + j * OUT : LANES + (j + 1) * OUT].astype(jnp.float32)
            one = (mine - smooth).astype(jnp.bfloat16)
            piece, inside = (j * OUT) // width, (j * OUT) % width
            cleaned[at * per + piece, :, inside : inside + OUT] = one
            done.append(one)
        total[...] += jnp.dot(
            jnp.concatenate(done, axis=1), tap[slot], preferred_element_type=jnp.float32
        )

    @pl.loop(0, tiles)
    def _(pos):
        clean(pos)

        @pl.when(pos + slots < tiles)
        def _():
            each_load(pos + slots, lambda c: c.start())

    @pl.when(mz < n_mz - 1)
    def _():
        to_right.wait_send()

    @pl.when(mz > 0)
    def _():
        to_left.wait_send()

    rows = parts.shape[1]
    for z in range(n_mz):
        parts[z] = total[z * rows : (z + 1) * rows]

    def scatter(d):
        return pltpu.make_async_remote_copy(
            src_ref=parts.at[lax.rem(mz + d, n_mz)], dst_ref=parts_in.at[d - 1],
            send_sem=parts_send.at[d - 1], recv_sem=parts_recv.at[d - 1],
            device_id=at_z(d), device_id_type=MESH,
        )

    for d in range(1, n_mz):
        scatter(d).start()
    mine = parts[mz]
    for d in range(1, n_mz):
        scatter(d).wait_recv()
        mine = mine + parts_in[d - 1]
    sketch[mz] = mine

    def gather(d, owner):
        return pltpu.make_async_remote_copy(
            src_ref=sketch.at[mz], dst_ref=sketch.at[owner],
            send_sem=all_send.at[d - 1], recv_sem=all_recv.at[d - 1],
            device_id=at_z(d), device_id_type=MESH,
        )

    for d in range(1, n_mz):
        gather(d, mz).start()
    for d in range(1, n_mz):
        gather(d, lax.rem(mz + n_mz - d, n_mz)).wait_recv()
    sk = jnp.concatenate([sketch[z] for z in range(n_mz)], axis=0)

    gram[...] = lax.dot_general(
        sk, sk, (((0,), (0,)), ((), ())), precision=HIGHEST, preferred_element_type=jnp.float32
    )

    def share_gram(d):
        return pltpu.make_async_remote_copy(
            src_ref=gram, dst_ref=gram_in.at[d - 1],
            send_sem=gram_send.at[d - 1], recv_sem=gram_recv.at[d - 1],
            device_id=at_pix(d), device_id_type=MESH,
        )

    for d in range(1, n_pix):
        share_gram(d).start()
    full = gram[...]
    for d in range(1, n_pix):
        share_gram(d).wait_recv()
        full = full + gram_in[d - 1]
    total[...] = full * (1.0 / pixels)
    whiten(total, x_ref)
    x = x_ref[...]
    by_lane = (((1,), (1,)), ((), ()))
    flipped = lax.dot_general(
        x, sk, by_lane, precision=HIGHEST, preferred_element_type=jnp.float32
    ).astype(jnp.bfloat16)
    basis_t = flipped.reshape(n_pix, share, flipped.shape[1])
    for chunk in range(n_pix):
        d = lax.rem(chunk // 2 - chip + chips, chips)
        at = d * share + jnp.where(core == chunk % 2, half, 0)
        lhs[pl.ds(pl.multiple_of(at, share), share), :] = basis_t[chunk]

    def to_core(k):
        return pltpu.make_async_remote_copy(
            src_ref=give.at[lax.rem(k, ring)], dst_ref=core_in.at[k],
            send_sem=give_sem.at[lax.rem(k, ring)], recv_sem=core_sem.at[k],
            device_id=device(chip, other), device_id_type=MESH,
        )

    def to_chip(d, k):
        return pltpu.make_async_remote_copy(
            src_ref=x_give.at[d - 1, k], dst_ref=x_in.at[d - 1, k],
            send_sem=x_send_sem.at[d - 1, k], recv_sem=x_recv_sem.at[d - 1, k],
            device_id=device(chip_of(d), core), device_id_type=MESH,
        )

    def first(k):
        slot = lax.rem(k, ring)

        @pl.when(k >= ring)
        def _():
            to_core(k - ring).wait_send()

        part = jnp.dot(lhs[...], cleaned[k], preferred_element_type=jnp.float32) * factor
        part = part.astype(jnp.bfloat16)
        give[slot] = part[:half]
        to_core(k).start()
        hold[slot] = part[half:]

    def second(k):
        to_core(k).wait_recv()
        slot = lax.rem(k, ring)
        added = hold[slot].astype(jnp.float32) + core_in[k].astype(jnp.float32)
        acc[k] = added[:share]
        for d in range(1, chips):
            x_give[d - 1, k] = added[d * share : (d + 1) * share].astype(jnp.bfloat16)
            to_chip(d, k).start()

    def store(k):
        slot = lax.rem(k, ring)
        return pltpu.make_async_copy(
            out_v.at[slot], out.at[:, pl.ds(pl.multiple_of(k * width, width), width)],
            store_sem.at[slot],
        )

    lag = min(ring - 1, chunks)

    @pl.loop(0, lag)
    def _(k):
        first(k)

    basis[...] = lax.dot_general(
        sk, x, by_lane, precision=HIGHEST, preferred_element_type=jnp.float32
    ).astype(jnp.bfloat16)

    @pl.loop(lag, chunks)
    def _(k):
        first(k)
        second(k - lag)

    @pl.loop(chunks - lag, chunks)
    def _(k):
        second(k)

    @pl.loop(max(chunks - ring, 0), chunks)
    def _(k):
        to_core(k).wait_send()

    for d in range(1, n_mz):
        scatter(d).wait_send()
        gather(d, mz).wait_send()
    for d in range(1, n_pix):
        share_gram(d).wait_send()

    @pl.loop(0, chunks)
    def _(k):
        added = acc[k]
        for d in range(1, chips):
            to_chip(d, k).wait()
            added = added + x_in[d - 1, k].astype(jnp.float32)

        @pl.when(k >= ring)
        def _():
            store(k - ring).wait()

        out_v[lax.rem(k, ring)] = added.astype(jnp.bfloat16)
        store(k).start()

    @pl.loop(max(chunks - ring, 0), chunks)
    def _(k):
        store(k).wait()


def per_device(spectra, kernel, probes):
    rows, bins = spectra.shape
    cols = probes.shape[1]
    n_pix, n_mz = lax.axis_size("pix"), lax.axis_size("mz")
    pixels = rows * n_pix
    factor = 1.0 / math.sqrt(float(pixels))
    taps = kernel.shape[0]
    low = WIN - (LANES - taps // 2) - (taps - 1)
    u = jnp.pad(kernel[::-1].astype(jnp.float32), (low, WIN - low - taps))[None, :]
    share = cols // n_pix
    chips = n_pix // 2
    half = chips * share
    tile = min(4096, bins // 2)
    width = min(2048, tile)
    chunks = bins // width
    slots, ring = 3, 4
    away = max(chips - 1, 1)
    part = rows // n_mz
    bf16, f32 = jnp.bfloat16, jnp.float32
    dma = pltpu.SemaphoreType.DMA
    return pl.pallas_call(
        functools.partial(fused_kernel, n_mz, n_pix, factor, float(pixels)),
        in_specs=[
            pl.BlockSpec(memory_space=pl.ANY),
            pl.BlockSpec(memory_space=pltpu.VMEM),
            pl.BlockSpec(memory_space=pl.ANY),
        ],
        out_specs=[pl.BlockSpec(memory_space=pltpu.VMEM), pl.BlockSpec(memory_space=pl.ANY)],
        out_shape=[
            jax.ShapeDtypeStruct((rows, cols), bf16),
            jax.ShapeDtypeStruct((share, bins), bf16),
        ],
        scratch_shapes=[
            pltpu.VMEM((slots, rows, tile + 2 * LANES), bf16),
            pltpu.VMEM((slots, tile, cols), bf16),
            pltpu.VMEM((WIN, OUT), bf16),
            pltpu.VMEM((2, rows, LANES), bf16),
            pltpu.VMEM((chunks, rows, width), bf16),
            pltpu.VMEM((rows, cols), f32),
            pltpu.VMEM((n_mz, part, cols), f32),
            pltpu.VMEM((n_mz - 1, part, cols), f32),
            pltpu.VMEM((n_mz, part, cols), f32),
            pltpu.VMEM((cols, cols), f32),
            pltpu.VMEM((n_pix - 1, cols, cols), f32),
            pltpu.VMEM((cols, cols), f32),
            pltpu.VMEM((cols, rows), bf16),
            pltpu.VMEM((ring, half, width), bf16),
            pltpu.VMEM((chunks, half, width), bf16),
            pltpu.VMEM((ring, half, width), bf16),
            pltpu.VMEM((away, chunks, share, width), bf16),
            pltpu.VMEM((away, chunks, share, width), bf16),
            pltpu.VMEM((chunks, share, width), f32),
            pltpu.VMEM((ring, share, width), bf16),
            dma((slots,)),
            dma((slots,)),
            dma((2,)),
            dma((2,)),
            dma((n_mz - 1,)),
            dma((n_mz - 1,)),
            dma((n_mz - 1,)),
            dma((n_mz - 1,)),
            dma((n_pix - 1,)),
            dma((n_pix - 1,)),
            dma((ring,)),
            dma((chunks,)),
            dma((away, chunks)),
            dma((away, chunks)),
            dma((ring,)),
        ],
        compiler_params=pltpu.CompilerParams(
            collective_id=0, has_side_effects=True, vmem_limit_bytes=58 * 2**20
        ),
        cost_estimate=pl.CostEstimate(
            flops=2 * rows * bins * (WIN + 2 * cols),
            bytes_accessed=2 * bins * (rows + cols + share),
            transcendentals=0,
        ),
    )(spectra, u, probes)


def solution(mesh):
    in_specs = (P(("groups", "pix"), "mz"), P(), P("mz", None))
    out_specs = (P(("groups", "pix"), None), P(("groups", "pix"), "mz"))
    return jax.shard_map(
        per_device, mesh=mesh, in_specs=in_specs, out_specs=out_specs, check_vma=False
    )
```

```python
import functools
import math

import jax
import jax.numpy as jnp
from jax import lax
from jax.experimental import pallas as pl
from jax.experimental.pallas import tpu as pltpu
from jax.sharding import PartitionSpec as P

LANES = 128
OUT = 256
WIN = OUT + 2 * LANES


MESH = pl.DeviceIdType.MESH
HIGHEST = lax.Precision.HIGHEST
PANEL = 8


def whiten(a_ref, x_ref):
    size = a_ref.shape[0]
    row = lax.broadcasted_iota(jnp.int32, (PANEL, 1), 0)
    a = a_ref[...]
    x = (
        lax.broadcasted_iota(jnp.int32, (size, size), 0)
        == lax.broadcasted_iota(jnp.int32, (size, size), 1)
    ).astype(jnp.float32)
    blocks = size // PANEL
    a = [a[i * PANEL : (i + 1) * PANEL] for i in range(blocks)]
    x = [x[i * PANEL : (i + 1) * PANEL] for i in range(blocks)]
    for index in range(blocks):
        p, q = a[index], x[index]
        rows_p, rows_q = [], []
        spread = [
            jnp.broadcast_to(p[:, index * PANEL + t : index * PANEL + t + 1], p.shape)
            for t in range(PANEL)
        ]
        for t in range(PANEL):
            inv = lax.rsqrt(spread[t][t : t + 1])
            r, y = p[t : t + 1] * inv, q[t : t + 1] * inv
            rows_p.append(r)
            rows_q.append(y)
            if t + 1 < PANEL:
                scale = jnp.where(row > t, spread[t] * inv, 0.0)
                p = p - scale * r
                q = q - scale * y
                for j in range(t + 1, PANEL):
                    spread[j] = spread[j] - scale * (spread[j][t : t + 1] * inv)
        x_ref[index * PANEL : (index + 1) * PANEL, :] = jnp.concatenate(rows_q, axis=0)
        if index + 1 < blocks:
            turned = jnp.concatenate(rows_p, axis=0).T
            for later in range(index + 1, blocks):
                for t in range(PANEL):
                    scale = turned[later * PANEL : (later + 1) * PANEL, t : t + 1]
                    a[later] = a[later] - scale * rows_p[t]
                    x[later] = x[later] - scale * rows_q[t]


def fused_kernel(
    n_mz, n_pix, factor, pixels, spectra, u_ref, probes, basis, out,
    raw, tap, w_ref, halo, cleaned, total, parts, parts_in, sketch, gram, gram_in, x_ref,
    lhs, give, core_in, hold, x_give, x_in, acc, out_v,
    raw_sem, tap_sem, halo_send, halo_recv, parts_send, parts_recv, all_send, all_recv,
    gram_send, gram_recv, give_sem, core_sem, x_send_sem, x_recv_sem, store_sem,
):
    bins = spectra.shape[1]
    slots, tile = tap.shape[0], tap.shape[1]
    tiles = bins // tile
    chips = n_pix // 2
    share = lhs.shape[0] // n_pix
    half = chips * share
    chunks, width = acc.shape[0], acc.shape[2]
    per = tile // width
    ring = give.shape[0]
    groups, mz, pix = lax.axis_index("groups"), lax.axis_index("mz"), lax.axis_index("pix")
    core = lax.rem(pix, 2)
    chip = lax.div(pix, 2)
    other = 1 - core

    def at_z(d):
        return (groups, lax.rem(mz + d, n_mz), pix)

    def at_pix(d):
        return (groups, mz, lax.rem(pix + d, n_pix))

    def device(at_chip, at_core):
        return (groups, mz, at_chip * 2 + at_core)

    def chip_of(d):
        return lax.rem(chip + d, chips)

    def tile_of(pos):
        return jnp.where(pos == tiles - 1, tiles - 1, jnp.where(pos == tiles - 2, 0, pos + 1))

    def each_load(pos, act):
        slot = lax.rem(pos, slots)

        @pl.when(pos < tiles - 2)
        def _():
            begin = pl.multiple_of((pos + 1) * tile - LANES, LANES)
            act(pltpu.make_async_copy(
                spectra.at[:, pl.ds(begin, tile + 2 * LANES)], raw.at[slot], raw_sem.at[slot]))

        @pl.when(pos == tiles - 2)
        def _():
            act(pltpu.make_async_copy(
                spectra.at[:, pl.ds(0, tile + LANES)],
                raw.at[slot, :, pl.ds(LANES, tile + LANES)], raw_sem.at[slot]))

        @pl.when(pos == tiles - 1)
        def _():
            act(pltpu.make_async_copy(
                spectra.at[:, pl.ds(bins - tile - LANES, tile + LANES)],
                raw.at[slot, :, pl.ds(0, tile + LANES)], raw_sem.at[slot]))

        begin = pl.multiple_of(tile_of(pos) * tile, tile)
        act(pltpu.make_async_copy(probes.at[pl.ds(begin, tile), :], tap.at[slot], tap_sem.at[slot]))

    for pos in range(min(slots, tiles)):
        each_load(jnp.int32(pos), lambda c: c.start())

    barrier = pltpu.get_barrier_semaphore()
    for d in range(1, n_mz):
        pl.semaphore_signal(barrier, inc=1, device_id=at_z(d), device_id_type=MESH)
    for d in range(1, n_pix):
        pl.semaphore_signal(barrier, inc=1, device_id=at_pix(d), device_id_type=MESH)

    base = jnp.broadcast_to(u_ref[...], (WIN, WIN))
    w_ref[...] = pltpu.roll(base, 0, 1, stride=1, stride_axis=0)[:, :OUT].astype(jnp.bfloat16)
    total[...] = jnp.zeros_like(total)

    pl.semaphore_wait(barrier, n_mz - 1 + n_pix - 1)

    to_right = pltpu.make_async_remote_copy(
        src_ref=spectra.at[:, pl.ds(bins - LANES, LANES)], dst_ref=halo.at[0],
        send_sem=halo_send.at[0], recv_sem=halo_recv.at[0],
        device_id=at_z(1), device_id_type=MESH,
    )
    to_left = pltpu.make_async_remote_copy(
        src_ref=spectra.at[:, pl.ds(0, LANES)], dst_ref=halo.at[1],
        send_sem=halo_send.at[1], recv_sem=halo_recv.at[1],
        device_id=at_z(n_mz - 1), device_id_type=MESH,
    )

    @pl.when(mz < n_mz - 1)
    def _():
        to_right.start()

    @pl.when(mz > 0)
    def _():
        to_left.start()

    @pl.when(mz == 0)
    def _():
        halo[0] = jnp.zeros(halo.shape[1:], halo.dtype)

    @pl.when(mz == n_mz - 1)
    def _():
        halo[1] = jnp.zeros(halo.shape[1:], halo.dtype)

    def clean(pos):
        slot = lax.rem(pos, slots)
        at = tile_of(pos)
        each_load(pos, lambda c: c.wait())

        @pl.when(pos == tiles - 2)
        def _():
            @pl.when(mz > 0)
            def _():
                to_right.wait_recv()

            raw[slot, :, :LANES] = halo[0]

        @pl.when(pos == tiles - 1)
        def _():
            @pl.when(mz < n_mz - 1)
            def _():
                to_left.wait_recv()

            raw[slot, :, tile + LANES :] = halo[1]

        w = w_ref[...]
        done = []
        for j in range(tile // OUT):
            window = raw[slot, :, j * OUT : j * OUT + WIN]
            smooth = jnp.dot(window, w, preferred_element_type=jnp.float32)
            mine = raw[slot, :, LANES + j * OUT : LANES + (j + 1) * OUT].astype(jnp.float32)
            one = (mine - smooth).astype(jnp.bfloat16)
            piece, inside = (j * OUT) // width, (j * OUT) % width
            cleaned[at * per + piece, :, inside : inside + OUT] = one
            done.append(one)
        total[...] += jnp.dot(
            jnp.concatenate(done, axis=1), tap[slot], preferred_element_type=jnp.float32
        )

    @pl.loop(0, tiles)
    def _(pos):
        clean(pos)

        @pl.when(pos + slots < tiles)
        def _():
            each_load(pos + slots, lambda c: c.start())

    @pl.when(mz < n_mz - 1)
    def _():
        to_right.wait_send()

    @pl.when(mz > 0)
    def _():
        to_left.wait_send()

    rows = parts.shape[1]
    for z in range(n_mz):
        parts[z] = total[z * rows : (z + 1) * rows]

    def scatter(d):
        return pltpu.make_async_remote_copy(
            src_ref=parts.at[lax.rem(mz + d, n_mz)], dst_ref=parts_in.at[d - 1],
            send_sem=parts_send.at[d - 1], recv_sem=parts_recv.at[d - 1],
            device_id=at_z(d), device_id_type=MESH,
        )

    for d in range(1, n_mz):
        scatter(d).start()
    mine = parts[mz]
    for d in range(1, n_mz):
        scatter(d).wait_recv()
        mine = mine + parts_in[d - 1]
    sketch[mz] = mine

    def gather(d, owner):
        return pltpu.make_async_remote_copy(
            src_ref=sketch.at[mz], dst_ref=sketch.at[owner],
            send_sem=all_send.at[d - 1], recv_sem=all_recv.at[d - 1],
            device_id=at_z(d), device_id_type=MESH,
        )

    for d in range(1, n_mz):
        gather(d, mz).start()
    for d in range(1, n_mz):
        gather(d, lax.rem(mz + n_mz - d, n_mz)).wait_recv()
    sk = jnp.concatenate([sketch[z] for z in range(n_mz)], axis=0)

    gram[...] = lax.dot_general(
        sk, sk, (((0,), (0,)), ((), ())), precision=HIGHEST, preferred_element_type=jnp.float32
    )

    def share_gram(d):
        return pltpu.make_async_remote_copy(
            src_ref=gram, dst_ref=gram_in.at[d - 1],
            send_sem=gram_send.at[d - 1], recv_sem=gram_recv.at[d - 1],
            device_id=at_pix(d), device_id_type=MESH,
        )

    for d in range(1, n_pix):
        share_gram(d).start()
    full = gram[...]
    for d in range(1, n_pix):
        share_gram(d).wait_recv()
        full = full + gram_in[d - 1]
    total[...] = full * (1.0 / pixels)
    whiten(total, x_ref)
    x = x_ref[...]
    by_lane = (((1,), (1,)), ((), ()))
    flipped = lax.dot_general(
        x, sk, by_lane, precision=HIGHEST, preferred_element_type=jnp.float32
    ).astype(jnp.bfloat16)
    basis_t = flipped.reshape(n_pix, share, flipped.shape[1])
    for chunk in range(n_pix):
        d = lax.rem(chunk // 2 - chip + chips, chips)
        at = d * share + jnp.where(core == chunk % 2, half, 0)
        lhs[pl.ds(pl.multiple_of(at, share), share), :] = basis_t[chunk]

    def to_core(k):
        return pltpu.make_async_remote_copy(
            src_ref=give.at[lax.rem(k, ring)], dst_ref=core_in.at[k],
            send_sem=give_sem.at[lax.rem(k, ring)], recv_sem=core_sem.at[k],
            device_id=device(chip, other), device_id_type=MESH,
        )

    def to_chip(d, k):
        return pltpu.make_async_remote_copy(
            src_ref=x_give.at[d - 1, k], dst_ref=x_in.at[d - 1, k],
            send_sem=x_send_sem.at[d - 1, k], recv_sem=x_recv_sem.at[d - 1, k],
            device_id=device(chip_of(d), core), device_id_type=MESH,
        )

    def first(k):
        slot = lax.rem(k, ring)

        @pl.when(k >= ring)
        def _():
            to_core(k - ring).wait_send()

        part = jnp.dot(lhs[...], cleaned[k], preferred_element_type=jnp.float32) * factor
        part = part.astype(jnp.bfloat16)
        give[slot] = part[:half]
        to_core(k).start()
        hold[slot] = part[half:]

    def second(k):
        to_core(k).wait_recv()
        slot = lax.rem(k, ring)
        added = hold[slot].astype(jnp.float32) + core_in[k].astype(jnp.float32)
        acc[k] = added[:share]
        for d in range(1, chips):
            x_give[d - 1, k] = added[d * share : (d + 1) * share].astype(jnp.bfloat16)
            to_chip(d, k).start()

    def store(k):
        slot = lax.rem(k, ring)
        return pltpu.make_async_copy(
            out_v.at[slot], out.at[:, pl.ds(pl.multiple_of(k * width, width), width)],
            store_sem.at[slot],
        )

    lag = min(ring - 1, chunks)

    @pl.loop(0, lag)
    def _(k):
        first(k)

    basis[...] = lax.dot_general(
        sk, x, by_lane, precision=HIGHEST, preferred_element_type=jnp.float32
    ).astype(jnp.bfloat16)

    @pl.loop(lag, chunks)
    def _(k):
        first(k)
        second(k - lag)

    @pl.loop(chunks - lag, chunks)
    def _(k):
        second(k)

    @pl.loop(max(chunks - ring, 0), chunks)
    def _(k):
        to_core(k).wait_send()

    for d in range(1, n_mz):
        scatter(d).wait_send()
        gather(d, mz).wait_send()
    for d in range(1, n_pix):
        share_gram(d).wait_send()

    @pl.loop(0, chunks)
    def _(k):
        added = acc[k]
        for d in range(1, chips):
            to_chip(d, k).wait()
            added = added + x_in[d - 1, k].astype(jnp.float32)

        @pl.when(k >= ring)
        def _():
            store(k - ring).wait()

        out_v[lax.rem(k, ring)] = added.astype(jnp.bfloat16)
        store(k).start()

    @pl.loop(max(chunks - ring, 0), chunks)
    def _(k):
        store(k).wait()


def per_device(spectra, kernel, probes):
    rows, bins = spectra.shape
    cols = probes.shape[1]
    n_pix, n_mz = lax.axis_size("pix"), lax.axis_size("mz")
    pixels = rows * n_pix
    factor = 1.0 / math.sqrt(float(pixels))
    taps = kernel.shape[0]
    low = WIN - (LANES - taps // 2) - (taps - 1)
    u = jnp.pad(kernel[::-1].astype(jnp.float32), (low, WIN - low - taps))[None, :]
    share = cols // n_pix
    chips = n_pix // 2
    half = chips * share
    tile = min(4096, bins // 2)
    width = min(2048, tile)
    chunks = bins // width
    slots, ring = 3, 4
    away = max(chips - 1, 1)
    part = rows // n_mz
    bf16, f32 = jnp.bfloat16, jnp.float32
    dma = pltpu.SemaphoreType.DMA
    return pl.pallas_call(
        functools.partial(fused_kernel, n_mz, n_pix, factor, float(pixels)),
        in_specs=[
            pl.BlockSpec(memory_space=pl.ANY),
            pl.BlockSpec(memory_space=pltpu.VMEM),
            pl.BlockSpec(memory_space=pl.ANY),
        ],
        out_specs=[pl.BlockSpec(memory_space=pltpu.VMEM), pl.BlockSpec(memory_space=pl.ANY)],
        out_shape=[
            jax.ShapeDtypeStruct((rows, cols), bf16),
            jax.ShapeDtypeStruct((share, bins), bf16),
        ],
        scratch_shapes=[
            pltpu.VMEM((slots, rows, tile + 2 * LANES), bf16),
            pltpu.VMEM((slots, tile, cols), bf16),
            pltpu.VMEM((WIN, OUT), bf16),
            pltpu.VMEM((2, rows, LANES), bf16),
            pltpu.VMEM((chunks, rows, width), bf16),
            pltpu.VMEM((rows, cols), f32),
            pltpu.VMEM((n_mz, part, cols), f32),
            pltpu.VMEM((n_mz - 1, part, cols), f32),
            pltpu.VMEM((n_mz, part, cols), f32),
            pltpu.VMEM((cols, cols), f32),
            pltpu.VMEM((n_pix - 1, cols, cols), f32),
            pltpu.VMEM((cols, cols), f32),
            pltpu.VMEM((cols, rows), bf16),
            pltpu.VMEM((ring, half, width), bf16),
            pltpu.VMEM((chunks, half, width), bf16),
            pltpu.VMEM((ring, half, width), bf16),
            pltpu.VMEM((away, chunks, share, width), bf16),
            pltpu.VMEM((away, chunks, share, width), bf16),
            pltpu.VMEM((chunks, share, width), f32),
            pltpu.VMEM((ring, share, width), bf16),
            dma((slots,)),
            dma((slots,)),
            dma((2,)),
            dma((2,)),
            dma((n_mz - 1,)),
            dma((n_mz - 1,)),
            dma((n_mz - 1,)),
            dma((n_mz - 1,)),
            dma((n_pix - 1,)),
            dma((n_pix - 1,)),
            dma((ring,)),
            dma((chunks,)),
            dma((away, chunks)),
            dma((away, chunks)),
            dma((ring,)),
        ],
        compiler_params=pltpu.CompilerParams(
            collective_id=0, has_side_effects=True, vmem_limit_bytes=58 * 2**20
        ),
        cost_estimate=pl.CostEstimate(
            flops=2 * rows * bins * (WIN + 2 * cols),
            bytes_accessed=2 * bins * (rows + cols + share),
            transcendentals=0,
        ),
    )(spectra, u, probes)


def solution(mesh):
    in_specs = (P(("groups", "pix"), "mz"), P(), P("mz", None))
    out_specs = (P(("groups", "pix"), None), P(("groups", "pix"), "mz"))
    return jax.shard_map(
        per_device, mesh=mesh, in_specs=in_specs, out_specs=out_specs, check_vma=False
    )
```

```python
import functools
import math

import jax
import jax.numpy as jnp
from jax import lax
from jax.experimental import pallas as pl
from jax.experimental.pallas import tpu as pltpu
from jax.sharding import PartitionSpec as P

LANES = 128
OUT = 256
WIN = OUT + 2 * LANES


MESH = pl.DeviceIdType.MESH
HIGHEST = lax.Precision.HIGHEST
PANEL = 8
EARLY = 3
AHEAD = 2


def whiten(a_ref, x_ref):
    size = a_ref.shape[0]
    row = lax.broadcasted_iota(jnp.int32, (PANEL, 1), 0)
    a = a_ref[...]
    x = (
        lax.broadcasted_iota(jnp.int32, (size, size), 0)
        == lax.broadcasted_iota(jnp.int32, (size, size), 1)
    ).astype(jnp.float32)
    blocks = size // PANEL
    a = [a[i * PANEL : (i + 1) * PANEL] for i in range(blocks)]
    x = [x[i * PANEL : (i + 1) * PANEL] for i in range(blocks)]
    for index in range(blocks):
        p, q = a[index], x[index]
        rows_p, rows_q = [], []
        spread = [
            jnp.broadcast_to(p[:, index * PANEL + t : index * PANEL + t + 1], p.shape)
            for t in range(PANEL)
        ]
        for t in range(PANEL):
            inv = lax.rsqrt(spread[t][t : t + 1])
            r, y = p[t : t + 1] * inv, q[t : t + 1] * inv
            rows_p.append(r)
            rows_q.append(y)
            if t + 1 < PANEL:
                scale = jnp.where(row > t, spread[t] * inv, 0.0)
                p = p - scale * r
                q = q - scale * y
                for j in range(t + 1, PANEL):
                    spread[j] = spread[j] - scale * (spread[j][t : t + 1] * inv)
        x_ref[index * PANEL : (index + 1) * PANEL, :] = jnp.concatenate(rows_q, axis=0)
        if index + 1 < blocks:
            turned = jnp.concatenate(rows_p, axis=0).T
            for later in range(index + 1, blocks):
                for t in range(PANEL):
                    scale = turned[later * PANEL : (later + 1) * PANEL, t : t + 1]
                    a[later] = a[later] - scale * rows_p[t]
                    x[later] = x[later] - scale * rows_q[t]


def fused_kernel(
    n_mz, n_pix, factor, pixels, early, ahead, spectra, u_ref, probes, basis, out,
    raw, tap, w_ref, halo, cleaned, total, parts, parts_in, sketch, gram, gram_in, x_ref,
    lhs, give, core_in, hold, x_give, x_in, acc, out_v, lhs_far, early_in, sketch_far,
    raw_sem, tap_sem, halo_send, halo_recv, parts_send, parts_recv, all_send, all_recv,
    gram_send, gram_recv, give_sem, core_sem, x_send_sem, x_recv_sem, store_sem,
    early_send, early_recv, far_send, far_recv,
):
    bins = spectra.shape[1]
    slots, tile = tap.shape[0], tap.shape[1]
    tiles = bins // tile
    chips = n_pix // 2
    share = lhs.shape[0] // n_pix
    half = chips * share
    chunks, width = acc.shape[0], acc.shape[2]
    per = tile // width
    ring = give.shape[0]
    groups, mz, pix = lax.axis_index("groups"), lax.axis_index("mz"), lax.axis_index("pix")
    core = lax.rem(pix, 2)
    chip = lax.div(pix, 2)
    other = 1 - core

    def at_z(d):
        return (groups, lax.rem(mz + d, n_mz), pix)

    def at_pix(d):
        return (groups, mz, lax.rem(pix + d, n_pix))

    def device(at_chip, at_core):
        return (groups, mz, at_chip * 2 + at_core)

    def chip_of(d):
        return lax.rem(chip + d, chips)

    def tile_of(pos):
        return jnp.where(pos == tiles - 1, tiles - 1, jnp.where(pos == tiles - 2, 0, pos + 1))

    def each_load(pos, act):
        slot = lax.rem(pos, slots)

        @pl.when(pos < tiles - 2)
        def _():
            begin = pl.multiple_of((pos + 1) * tile - LANES, LANES)
            act(pltpu.make_async_copy(
                spectra.at[:, pl.ds(begin, tile + 2 * LANES)], raw.at[slot], raw_sem.at[slot]))

        @pl.when(pos == tiles - 2)
        def _():
            act(pltpu.make_async_copy(
                spectra.at[:, pl.ds(0, tile + LANES)],
                raw.at[slot, :, pl.ds(LANES, tile + LANES)], raw_sem.at[slot]))

        @pl.when(pos == tiles - 1)
        def _():
            act(pltpu.make_async_copy(
                spectra.at[:, pl.ds(bins - tile - LANES, tile + LANES)],
                raw.at[slot, :, pl.ds(0, tile + LANES)], raw_sem.at[slot]))

        begin = pl.multiple_of(tile_of(pos) * tile, tile)
        act(pltpu.make_async_copy(probes.at[pl.ds(begin, tile), :], tap.at[slot], tap_sem.at[slot]))

    both = chunks - 2 * early

    def whole_of(e, at_chip):
        return per + 2 * e + at_chip

    def chunk_of(i):
        return jnp.where(i < per, i, jnp.where(
            i < both, i + 2 * early, whole_of(i - both, chip)))

    def send_early(e):
        return pltpu.make_async_remote_copy(
            src_ref=cleaned.at[whole_of(e, 1 - chip)], dst_ref=early_in.at[e],
            send_sem=early_send.at[e], recv_sem=early_recv.at[e],
            device_id=device(1 - chip, core), device_id_type=MESH,
        )

    for pos in range(min(slots, tiles)):
        each_load(jnp.int32(pos), lambda c: c.start())

    barrier = pltpu.get_barrier_semaphore()
    for d in range(1, n_mz):
        pl.semaphore_signal(barrier, inc=1, device_id=at_z(d), device_id_type=MESH)
    for d in range(1, n_pix):
        pl.semaphore_signal(barrier, inc=1, device_id=at_pix(d), device_id_type=MESH)

    base = jnp.broadcast_to(u_ref[...], (WIN, WIN))
    w_ref[...] = pltpu.roll(base, 0, 1, stride=1, stride_axis=0)[:, :OUT].astype(jnp.bfloat16)
    total[...] = jnp.zeros_like(total)

    pl.semaphore_wait(barrier, n_mz - 1 + n_pix - 1)

    to_right = pltpu.make_async_remote_copy(
        src_ref=spectra.at[:, pl.ds(bins - LANES, LANES)], dst_ref=halo.at[0],
        send_sem=halo_send.at[0], recv_sem=halo_recv.at[0],
        device_id=at_z(1), device_id_type=MESH,
    )
    to_left = pltpu.make_async_remote_copy(
        src_ref=spectra.at[:, pl.ds(0, LANES)], dst_ref=halo.at[1],
        send_sem=halo_send.at[1], recv_sem=halo_recv.at[1],
        device_id=at_z(n_mz - 1), device_id_type=MESH,
    )

    @pl.when(mz < n_mz - 1)
    def _():
        to_right.start()

    @pl.when(mz > 0)
    def _():
        to_left.start()

    @pl.when(mz == 0)
    def _():
        halo[0] = jnp.zeros(halo.shape[1:], halo.dtype)

    @pl.when(mz == n_mz - 1)
    def _():
        halo[1] = jnp.zeros(halo.shape[1:], halo.dtype)

    def clean(pos):
        slot = lax.rem(pos, slots)
        at = tile_of(pos)
        each_load(pos, lambda c: c.wait())

        @pl.when(pos == tiles - 2)
        def _():
            @pl.when(mz > 0)
            def _():
                to_right.wait_recv()

            raw[slot, :, :LANES] = halo[0]

        @pl.when(pos == tiles - 1)
        def _():
            @pl.when(mz < n_mz - 1)
            def _():
                to_left.wait_recv()

            raw[slot, :, tile + LANES :] = halo[1]

        w = w_ref[...]
        done = []
        for j in range(tile // OUT):
            window = raw[slot, :, j * OUT : j * OUT + WIN]
            smooth = jnp.dot(window, w, preferred_element_type=jnp.float32)
            mine = raw[slot, :, LANES + j * OUT : LANES + (j + 1) * OUT].astype(jnp.float32)
            one = (mine - smooth).astype(jnp.bfloat16)
            piece, inside = (j * OUT) // width, (j * OUT) % width
            cleaned[at * per + piece, :, inside : inside + OUT] = one
            done.append(one)
        total[...] += jnp.dot(
            jnp.concatenate(done, axis=1), tap[slot], preferred_element_type=jnp.float32
        )

    @pl.loop(0, tiles)
    def _(pos):
        clean(pos)

        @pl.when(pos + slots < tiles)
        def _():
            each_load(pos + slots, lambda c: c.start())

        if ahead:
            @pl.when(pos < ahead)
            def _():
                send_early(pos).start()

    @pl.when(mz < n_mz - 1)
    def _():
        to_right.wait_send()

    @pl.when(mz > 0)
    def _():
        to_left.wait_send()

    rows = parts.shape[1]
    for z in range(n_mz):
        parts[z] = total[z * rows : (z + 1) * rows]

    def scatter(d):
        return pltpu.make_async_remote_copy(
            src_ref=parts.at[lax.rem(mz + d, n_mz)], dst_ref=parts_in.at[d - 1],
            send_sem=parts_send.at[d - 1], recv_sem=parts_recv.at[d - 1],
            device_id=at_z(d), device_id_type=MESH,
        )

    for d in range(1, n_mz):
        scatter(d).start()
    mine = parts[mz]
    for d in range(1, n_mz):
        scatter(d).wait_recv()
        mine = mine + parts_in[d - 1]
    sketch[mz] = mine

    def gather(d, owner):
        return pltpu.make_async_remote_copy(
            src_ref=sketch.at[mz], dst_ref=sketch.at[owner],
            send_sem=all_send.at[d - 1], recv_sem=all_recv.at[d - 1],
            device_id=at_z(d), device_id_type=MESH,
        )

    for d in range(1, n_mz):
        gather(d, mz).start()
    for d in range(1, n_mz):
        gather(d, lax.rem(mz + n_mz - d, n_mz)).wait_recv()
    sk = jnp.concatenate([sketch[z] for z in range(n_mz)], axis=0)

    gram[...] = lax.dot_general(
        sk, sk, (((0,), (0,)), ((), ())), precision=HIGHEST, preferred_element_type=jnp.float32
    )

    def share_gram(d):
        return pltpu.make_async_remote_copy(
            src_ref=gram, dst_ref=gram_in.at[d - 1],
            send_sem=gram_send.at[d - 1], recv_sem=gram_recv.at[d - 1],
            device_id=at_pix(d), device_id_type=MESH,
        )

    for d in range(1, n_pix):
        share_gram(d).start()
    to_far = pltpu.make_async_remote_copy(
        src_ref=sketch, dst_ref=sketch_far, send_sem=far_send.at[0], recv_sem=far_recv.at[0],
        device_id=device(1 - chip, core), device_id_type=MESH,
    )
    if early:
        to_far.start()
    full = gram[...]
    for d in range(1, n_pix):
        share_gram(d).wait_recv()
        full = full + gram_in[d - 1]
    if early:
        to_far.wait_recv()
        for e in range(ahead, early):
            send_early(e).start()
    total[...] = full * (1.0 / pixels)
    whiten(total, x_ref)
    x = x_ref[...]
    by_lane = (((1,), (1,)), ((), ()))

    def fill(target, of):
        flipped = lax.dot_general(
            x, of, by_lane, precision=HIGHEST, preferred_element_type=jnp.float32
        ).astype(jnp.bfloat16)
        basis_t = flipped.reshape(n_pix, share, flipped.shape[1])
        for chunk in range(n_pix):
            d = lax.rem(chunk // 2 - chip + chips, chips)
            at = d * share + jnp.where(core == chunk % 2, half, 0)
            target[pl.ds(pl.multiple_of(at, share), share), :] = basis_t[chunk]

    fill(lhs, sk)

    def to_core(k):
        return pltpu.make_async_remote_copy(
            src_ref=give.at[lax.rem(k, ring)], dst_ref=core_in.at[k],
            send_sem=give_sem.at[lax.rem(k, ring)], recv_sem=core_sem.at[k],
            device_id=device(chip, other), device_id_type=MESH,
        )

    def to_chip(d, k):
        return pltpu.make_async_remote_copy(
            src_ref=x_give.at[d - 1, k], dst_ref=x_in.at[d - 1, k],
            send_sem=x_send_sem.at[d - 1, k], recv_sem=x_recv_sem.at[d - 1, k],
            device_id=device(chip_of(d), core), device_id_type=MESH,
        )

    def product(left, right):
        part = jnp.dot(left, right, preferred_element_type=jnp.float32) * factor
        return part.astype(jnp.bfloat16)

    def first(i, alone):
        slot = lax.rem(i, ring)

        @pl.when(i >= ring)
        def _():
            to_core(i - ring).wait_send()

        part = product(lhs[...], cleaned[chunk_of(i)])
        if alone:
            send_early(i - both).wait_recv()
            far = product(lhs_far[...], early_in[i - both])
            part = (part.astype(jnp.float32) + far.astype(jnp.float32)).astype(jnp.bfloat16)
        give[slot] = part[:half]
        to_core(i).start()
        hold[slot] = part[half:]

    def second(i):
        to_core(i).wait_recv()
        slot = lax.rem(i, ring)
        k = chunk_of(i)
        added = hold[slot].astype(jnp.float32) + core_in[i].astype(jnp.float32)
        acc[k] = added[:share]
        for d in range(1, chips):
            x_give[d - 1, k] = added[d * share : (d + 1) * share].astype(jnp.bfloat16)
            to_chip(d, k).start()

    def store(n, k):
        slot = lax.rem(n, ring)
        return pltpu.make_async_copy(
            out_v.at[slot], out.at[:, pl.ds(pl.multiple_of(k * width, width), width)],
            store_sem.at[slot],
        )

    def emit(n, k, value):
        @pl.when(n >= ring)
        def _():
            store(n - ring, k).wait()

        out_v[lax.rem(n, ring)] = value.astype(jnp.bfloat16)
        store(n, k).start()

    lag = min(ring - 1, both)
    mine = chunks - early

    @pl.loop(0, lag)
    def _(i):
        first(i, False)

    basis[...] = lax.dot_general(
        sk, x, by_lane, precision=HIGHEST, preferred_element_type=jnp.float32
    ).astype(jnp.bfloat16)

    @pl.loop(lag, both)
    def _(i):
        first(i, False)
        second(i - lag)

    if early:
        fill(lhs_far, jnp.concatenate([sketch_far[z] for z in range(n_mz)], axis=0))

        @pl.loop(both, mine)
        def _(i):
            first(i, True)
            second(i - lag)

    @pl.loop(mine - lag, mine)
    def _(i):
        second(i)

    @pl.loop(max(mine - ring, 0), mine)
    def _(i):
        to_core(i).wait_send()

    for d in range(1, n_mz):
        scatter(d).wait_send()
        gather(d, mz).wait_send()
    for d in range(1, n_pix):
        share_gram(d).wait_send()
    if early:
        to_far.wait_send()
        for e in range(early):
            send_early(e).wait_send()

        @pl.loop(0, early)
        def _(e):
            emit(e, whole_of(e, chip), acc[whole_of(e, chip)])

    @pl.loop(0, both)
    def _(i):
        k = chunk_of(i)
        added = acc[k]
        for d in range(1, chips):
            to_chip(d, k).wait()
            added = added + x_in[d - 1, k].astype(jnp.float32)
        emit(early + i, k, added)

    if early:
        @pl.loop(0, early)
        def _(e):
            k = whole_of(e, 1 - chip)
            to_chip(1, k).wait_recv()
            emit(early + both + e, k, x_in[0, k])
            to_chip(1, whole_of(e, chip)).wait_send()

    @pl.loop(max(chunks - ring, 0), chunks)
    def _(n):
        store(n, n).wait()


def per_device(spectra, kernel, probes):
    rows, bins = spectra.shape
    cols = probes.shape[1]
    n_pix, n_mz = lax.axis_size("pix"), lax.axis_size("mz")
    pixels = rows * n_pix
    factor = 1.0 / math.sqrt(float(pixels))
    taps = kernel.shape[0]
    low = WIN - (LANES - taps // 2) - (taps - 1)
    u = jnp.pad(kernel[::-1].astype(jnp.float32), (low, WIN - low - taps))[None, :]
    share = cols // n_pix
    chips = n_pix // 2
    half = chips * share
    tile = min(4096, bins // 2)
    width = min(2048, tile)
    chunks = bins // width
    slots, ring = 3, 4
    fits = chips == 2 and tile == 2 * width and bins // tile >= 8
    early, ahead = (EARLY, AHEAD) if fits else (0, 0)
    kept = max(early, 1)
    away = max(chips - 1, 1)
    part = rows // n_mz
    bf16, f32 = jnp.bfloat16, jnp.float32
    dma = pltpu.SemaphoreType.DMA
    return pl.pallas_call(
        functools.partial(fused_kernel, n_mz, n_pix, factor, float(pixels), early, ahead),
        in_specs=[
            pl.BlockSpec(memory_space=pl.ANY),
            pl.BlockSpec(memory_space=pltpu.VMEM),
            pl.BlockSpec(memory_space=pl.ANY),
        ],
        out_specs=[pl.BlockSpec(memory_space=pltpu.VMEM), pl.BlockSpec(memory_space=pl.ANY)],
        out_shape=[
            jax.ShapeDtypeStruct((rows, cols), bf16),
            jax.ShapeDtypeStruct((share, bins), bf16),
        ],
        scratch_shapes=[
            pltpu.VMEM((slots, rows, tile + 2 * LANES), bf16),
            pltpu.VMEM((slots, tile, cols), bf16),
            pltpu.VMEM((WIN, OUT), bf16),
            pltpu.VMEM((2, rows, LANES), bf16),
            pltpu.VMEM((chunks, rows, width), bf16),
            pltpu.VMEM((rows, cols), f32),
            pltpu.VMEM((n_mz, part, cols), f32),
            pltpu.VMEM((n_mz - 1, part, cols), f32),
            pltpu.VMEM((n_mz, part, cols), f32),
            pltpu.VMEM((cols, cols), f32),
            pltpu.VMEM((n_pix - 1, cols, cols), f32),
            pltpu.VMEM((cols, cols), f32),
            pltpu.VMEM((cols, rows), bf16),
            pltpu.VMEM((ring, half, width), bf16),
            pltpu.VMEM((chunks, half, width), bf16),
            pltpu.VMEM((ring, half, width), bf16),
            pltpu.VMEM((away, chunks, share, width), bf16),
            pltpu.VMEM((away, chunks, share, width), bf16),
            pltpu.VMEM((chunks, share, width), f32),
            pltpu.VMEM((ring, share, width), bf16),
            pltpu.VMEM((cols, rows), bf16),
            pltpu.VMEM((kept, rows, width), bf16),
            pltpu.VMEM((n_mz, part, cols), f32),
            dma((slots,)),
            dma((slots,)),
            dma((2,)),
            dma((2,)),
            dma((n_mz - 1,)),
            dma((n_mz - 1,)),
            dma((n_mz - 1,)),
            dma((n_mz - 1,)),
            dma((n_pix - 1,)),
            dma((n_pix - 1,)),
            dma((ring,)),
            dma((chunks,)),
            dma((away, chunks)),
            dma((away, chunks)),
            dma((ring,)),
            dma((kept,)),
            dma((kept,)),
            dma((1,)),
            dma((1,)),
        ],
        compiler_params=pltpu.CompilerParams(
            collective_id=0, has_side_effects=True, vmem_limit_bytes=58 * 2**20
        ),
        cost_estimate=pl.CostEstimate(
            flops=2 * rows * bins * (WIN + 2 * cols),
            bytes_accessed=2 * bins * (rows + cols + share),
            transcendentals=0,
        ),
    )(spectra, u, probes)


def solution(mesh):
    in_specs = (P(("groups", "pix"), "mz"), P(), P("mz", None))
    out_specs = (P(("groups", "pix"), None), P(("groups", "pix"), "mz"))
    return jax.shard_map(
        per_device, mesh=mesh, in_specs=in_specs, out_specs=out_specs, check_vma=False
    )
```
